32 devices in a mesh: grp: 4 (over x, core), chan: 4 (over z), tile: 2 (over y).
Axes of the slice: x: 2, y: 2, z: 4, core: 2. Of those that a mesh axis runs over, the one named last changes fastest.
Arguments:
- voltages: bfloat16 [1024, 128, 2, 1024], P(('grp', 'tile'), 'chan'), may hold values from -6 to 6
- taps: float32 [8, 1024], replicated, may hold values from -0.0625 to 0.0625
Outputs:
- vis_real: float32 [64, 36, 128, 128], P(('grp', 'chan', 'tile'))
- vis_imag: float32 [64, 36, 128, 128], P(('grp', 'chan', 'tile'))
The draws below stay inside these ranges and needn't reach their ends.
All inputs are finite; a program needn't handle non-finite values.
Results may differ from the reference program's by a relative error of at most 0.004.
Values may be sent and summed in bfloat16 or wider, within the bound.
A program may use at most 256 MiB of HBM per device.

```python
import math
import jax
import jax.numpy as jnp
from jax import lax

ANTENNA_COUNT = 1024
FRAME_SAMPLES = 1024
FILTER_TAPS = 8
ANTENNA_BLOCKS = 8
SPECTRA_COUNT = 128
KEPT_CHANNELS = 64
TILE_ANTENNAS = 128


def level_of(rng, shape, cuts, least, largest):
    def one(position, shards_of):
        draws = jax.random.uniform(jax.random.fold_in(jax.random.fold_in(rng, 6), position), (shards_of,), jnp.float32, least / len(cuts), largest / len(cuts))
        return jnp.repeat(jnp.exp(draws), shape[position] // shards_of).reshape((-1,) + (1,) * (len(shape) - position - 1))

    level = one(*cuts[0])
    for cut in cuts[1:]:
        level = level * one(*cut)
    return level


def bell_draw(own_key, shape, spread, most, pieces=(), held_as=jnp.bfloat16):
    array = jax.random.normal(own_key, shape, jnp.float32) * spread
    if len(pieces) > 0:
        array = level_of(own_key, shape, pieces, -0.22, 0.18) * array
    return jnp.clip(array, min=-most, max=most).astype(held_as)


def setup_inputs(seed: int = 0) -> dict:
    keys = jax.random.split(jax.random.key(seed), 3)
    voltages = bell_draw(keys[0], (ANTENNA_COUNT, SPECTRA_COUNT, 2, FRAME_SAMPLES), 1.0, 6.0, ((0, 8), (1, 4)))
    taps = bell_draw(keys[1], (FILTER_TAPS, FRAME_SAMPLES), (FILTER_TAPS * FRAME_SAMPLES) ** -0.5, 0.0625, (), jnp.float32)
    return dict(voltages=voltages, taps=taps)


def transform_table(length, window):
    sample = jnp.arange(length, dtype=jnp.int32)[:, None]
    channel = jnp.arange(window, dtype=jnp.int32)[None, :]
    angles = ((sample * channel) % length).astype(jnp.float32) * (2.0 * math.pi / length)
    cosine = jnp.cos(angles)
    sine_part = jnp.sin(angles)
    upper_half = jnp.concatenate([cosine, -sine_part], axis=1)
    bottom = jnp.concatenate([sine_part, cosine], axis=1)
    return jnp.concatenate([upper_half, bottom], axis=0)


def split_into_channels(antenna_block, taps, fourier_transform):
    padded_samples = jnp.pad(antenna_block, ((0, 0), (FILTER_TAPS - 1, 0), (0, 0), (0, 0)))
    running_total = jnp.zeros(antenna_block.shape, jnp.float32)
    for tap_index in range(FILTER_TAPS):
        offset_frame = FILTER_TAPS - 1 - tap_index
        frames = padded_samples[:, offset_frame:offset_frame + SPECTRA_COUNT].astype(jnp.float32)
        running_total = running_total + taps[tap_index][None, None, None, :] * frames
    frame_matrix = running_total.reshape(-1, 2 * FRAME_SAMPLES)
    spectra_stack = jnp.dot(frame_matrix, fourier_transform, preferred_element_type=jnp.float32, precision=lax.Precision.HIGHEST).astype(jnp.bfloat16)
    return spectra_stack.reshape(antenna_block.shape[0], SPECTRA_COUNT, 2 * KEPT_CHANNELS)


def upper_tile_list(matrix):
    blocked = matrix.reshape(ANTENNA_BLOCKS, TILE_ANTENNAS, ANTENNA_BLOCKS, TILE_ANTENNAS).transpose(0, 2, 1, 3)
    return jnp.concatenate([blocked[row_block, row_block:] for row_block in range(ANTENNA_BLOCKS)], axis=0)


def correlate(channel_matrix):
    swapped = jnp.concatenate([channel_matrix[:, SPECTRA_COUNT:], -channel_matrix[:, :SPECTRA_COUNT]], axis=1)
    stacked_rows = jnp.concatenate([channel_matrix, swapped], axis=0)
    cross_products = jnp.dot(stacked_rows, channel_matrix.T, preferred_element_type=jnp.float32) * (1.0 / SPECTRA_COUNT)
    return upper_tile_list(cross_products[:ANTENNA_COUNT]), upper_tile_list(cross_products[ANTENNA_COUNT:])


def reference(voltages, taps):
    fourier_transform = transform_table(FRAME_SAMPLES, KEPT_CHANNELS)
    antenna_blocks = voltages.reshape(ANTENNA_BLOCKS, TILE_ANTENNAS, SPECTRA_COUNT, 2, FRAME_SAMPLES)
    spectra_stack = lax.map(lambda antenna_block: split_into_channels(antenna_block, taps, fourier_transform), antenna_blocks)
    spectra_stack = lax.optimization_barrier(spectra_stack.reshape(ANTENNA_COUNT, SPECTRA_COUNT, 2, KEPT_CHANNELS))
    channel_wise = spectra_stack.transpose(3, 0, 2, 1).reshape(KEPT_CHANNELS, ANTENNA_COUNT, 2 * SPECTRA_COUNT)
    vis_real, vis_imag = lax.map(correlate, channel_wise)
    return (vis_real, vis_imag)
```

```python
import functools

import jax
import jax.numpy as jnp
import numpy as np
from jax import lax
from jax.experimental import pallas as pl
from jax.experimental.pallas import tpu as pltpu
from jax.sharding import PartitionSpec as P

FRAME_SAMPLES = 1024
FILTER_TAPS = 8
CHUNK_FRAMES = 4
RIM_CHUNKS = 2
TILE_ANTENNAS = 128
LANES = 128
VMEM_LIMIT = 56 * 2**20


def transform_table(length, window):
    turns = np.arange(length)[:, None] * np.arange(window)[None, :] % length
    angles = turns * (2.0 * np.pi / length)
    return np.concatenate([np.cos(angles), np.sin(angles)], axis=1).astype(np.float32)


def regroup_matrix(window, devices):
    each = window // devices
    source = np.arange(2 * window).reshape(2, devices, each).transpose(1, 2, 0).reshape(-1)
    return np.eye(2 * window, dtype=np.float32)[source]


def filterbank_kernel(taps_ref, table_ref, volts_ref, out_ref, high, low, rows, total):
    step = pl.program_id(0)
    chunks = pl.num_programs(0) - RIM_CHUNKS
    antennas = volts_ref.shape[0]
    width = table_ref.shape[1]
    frame_rows = 2 * antennas
    chunk_rows = CHUNK_FRAMES * frame_rows

    @pl.when(step == 0)
    def _():
        total[...] = jnp.zeros_like(total)
        for tap in range(FILTER_TAPS):
            weights = taps_ref[:, tap : tap + 1] * table_ref[...]
            upper = weights.astype(jnp.bfloat16)
            columns = pl.ds(tap * width, width)
            high[:, columns] = upper
            low[:, columns] = (weights - upper.astype(jnp.float32)).astype(jnp.bfloat16)

    chunk = chunks - 1 - step

    @pl.when(chunk >= 0)
    def _():
        for frame in range(CHUNK_FRAMES):
            rows[pl.ds(frame * frame_rows, frame_rows), :] = volts_ref[:, frame].reshape(
                frame_rows, FRAME_SAMPLES
            )
        for pair in range(FILTER_TAPS // 2):
            columns = pl.ds(2 * pair * width, 2 * width)
            product = jnp.dot(
                rows[...], high[:, columns], preferred_element_type=jnp.float32
            ) + jnp.dot(rows[...], low[:, columns], preferred_element_type=jnp.float32)
            for part in range(2):
                first = (chunk * CHUNK_FRAMES + 2 * pair + part) * frame_rows
                place = pl.ds(pl.multiple_of(first, frame_rows), chunk_rows)
                for lanes in range(width // LANES):
                    begin = part * width + lanes * LANES
                    total[lanes, place, :] += product[:, begin : begin + LANES]

    half = chunk_rows // 2
    first = pl.multiple_of((chunk + RIM_CHUNKS) * chunk_rows, chunk_rows)

    def every_other(offset):
        place = pl.ds(first + offset, half, stride=2)
        return jnp.concatenate([total[i, place, :] for i in range(width // LANES)], axis=1)

    real, imaginary = every_other(0), every_other(1)
    lane = lax.broadcasted_iota(jnp.int32, (half, width), 1)
    signed = jnp.where(lane < width // 2, real, -real)
    out_ref[...] = signed + pltpu.roll(imaginary, width // 2, 1)


def filterbank(voltages, taps, table):
    antennas, frames = voltages.shape[:2]
    width = table.shape[1]
    chunks = frames // CHUNK_FRAMES
    padded = frames + RIM_CHUNKS * CHUNK_FRAMES
    return pl.pallas_call(
        filterbank_kernel,
        grid=(chunks + RIM_CHUNKS,),
        out_shape=jax.ShapeDtypeStruct((padded * antennas, width), jnp.float32),
        in_specs=[
            pl.BlockSpec((FRAME_SAMPLES, FILTER_TAPS), lambda i: (0, 0)),
            pl.BlockSpec((FRAME_SAMPLES, width), lambda i: (0, 0)),
            pl.BlockSpec(
                (antennas, CHUNK_FRAMES, 2, FRAME_SAMPLES),
                lambda i: (0, jnp.maximum(chunks - 1 - i, 0), 0, 0),
            ),
        ],
        out_specs=pl.BlockSpec(
            (CHUNK_FRAMES * antennas, width), lambda i: (chunks + RIM_CHUNKS - 1 - i, 0)
        ),
        scratch_shapes=[
            pltpu.VMEM((FRAME_SAMPLES, FILTER_TAPS * width), jnp.bfloat16),
            pltpu.VMEM((FRAME_SAMPLES, FILTER_TAPS * width), jnp.bfloat16),
            pltpu.VMEM((CHUNK_FRAMES * 2 * antennas, FRAME_SAMPLES), jnp.bfloat16),
            pltpu.VMEM((width // LANES, padded * 2 * antennas, LANES), jnp.float32),
        ],
        compiler_params=pltpu.CompilerParams(vmem_limit_bytes=VMEM_LIMIT),
    )(taps.T, table, voltages)


def regroup_kernel(order_ref, spectra_ref, rim_ref, out_ref):
    rim_rows = rim_ref.shape[0]
    rows = spectra_ref.shape[0]

    def put(first, block):
        out_ref[:, first : first + rim_rows] = lax.dot_general(
            order_ref[...],
            block.astype(jnp.bfloat16),
            (((1,), (1,)), ((), ())),
            preferred_element_type=jnp.float32,
        ).astype(jnp.bfloat16)

    put(0, spectra_ref[:rim_rows] + rim_ref[...])
    for first in range(rim_rows, rows, rim_rows):
        put(first, spectra_ref[first : first + rim_rows])


def regroup(order, spectra, rim, rows):
    width = order.shape[0]
    whole = lambda shape: pl.BlockSpec(shape, lambda i: (0, 0))
    return pl.pallas_call(
        regroup_kernel,
        grid=(1,),
        out_shape=jax.ShapeDtypeStruct((width, rows), jnp.bfloat16),
        in_specs=[whole(order.shape), whole((rows, width)), whole(rim.shape)],
        out_specs=whole((width, rows)),
        compiler_params=pltpu.CompilerParams(vmem_limit_bytes=VMEM_LIMIT),
    )(order, spectra, rim)


def correlate_kernel(scale, blocks, channel_ref, real_ref, imaginary_ref):
    depth = channel_ref.shape[1]
    matrix = channel_ref[0]
    swapped = jnp.concatenate([matrix[depth // 2 :], -matrix[: depth // 2]], axis=0)
    pair = 0
    for i in range(blocks):
        here = slice(i * TILE_ANTENNAS, (i + 1) * TILE_ANTENNAS)
        left = jnp.concatenate([matrix[:, here], swapped[:, here]], axis=1)
        product = (
            lax.dot_general(
                left,
                matrix[:, i * TILE_ANTENNAS :],
                (((0,), (0,)), ((), ())),
                preferred_element_type=jnp.float32,
            )
            * scale
        )
        for j in range(blocks - i):
            there = slice(j * TILE_ANTENNAS, (j + 1) * TILE_ANTENNAS)
            real_ref[0, pair] = product[:TILE_ANTENNAS, there]
            imaginary_ref[0, pair] = product[TILE_ANTENNAS:, there]
            pair += 1


def correlate(channel_matrix, scale):
    channels, depth, antennas = channel_matrix.shape
    blocks = antennas // TILE_ANTENNAS
    pairs = blocks * (blocks + 1) // 2
    tiles = jax.ShapeDtypeStruct((channels, pairs, TILE_ANTENNAS, TILE_ANTENNAS), jnp.float32)
    tile_spec = pl.BlockSpec((1, pairs, TILE_ANTENNAS, TILE_ANTENNAS), lambda c: (c, 0, 0, 0))
    return pl.pallas_call(
        functools.partial(correlate_kernel, scale, blocks),
        grid=(channels,),
        out_shape=(tiles, tiles),
        in_specs=[pl.BlockSpec((1, depth, antennas), lambda c: (c, 0, 0))],
        out_specs=(tile_spec, tile_spec),
        compiler_params=pltpu.CompilerParams(vmem_limit_bytes=VMEM_LIMIT),
    )(channel_matrix)


def on_device(each, voltages, taps):
    antennas, frames = voltages.shape[:2]
    groups, times, tiles = (lax.axis_size(axis) for axis in ("grp", "chan", "tile"))
    devices = groups * times * tiles
    window = each * devices
    table = jnp.asarray(transform_table(FRAME_SAMPLES, window))
    order = jnp.asarray(regroup_matrix(window, devices), jnp.bfloat16)
    spectra = filterbank(voltages, taps, table)
    rows = frames * antennas
    rim = lax.ppermute(spectra[rows:], "chan", [(i, i + 1) for i in range(times - 1)])
    leaving = regroup(order, spectra, rim, rows).reshape(devices, 2 * each, rows)
    received = lax.all_to_all(
        leaving, ("grp", "chan", "tile"), split_axis=0, concat_axis=0, tiled=True
    )
    received = received.reshape(groups, times, tiles, each, 2, frames, antennas)
    channel_matrix = received.transpose(3, 4, 1, 5, 0, 2, 6).reshape(
        each, 2 * times * frames, groups * tiles * antennas
    )
    return correlate(channel_matrix, 1.0 / (times * frames))


def solution(mesh):
    split = ("grp", "chan", "tile")
    return jax.shard_map(
        functools.partial(on_device, 2),
        mesh=mesh,
        in_specs=(P(("grp", "tile"), "chan", None, None), P()),
        out_specs=(P(split, None, None, None), P(split, None, None, None)),
        check_vma=False,
    )
```

```python
import functools
import math

import jax
import jax.numpy as jnp
import numpy as np
from jax import lax
from jax.experimental import pallas as pl
from jax.experimental.pallas import tpu as pltpu
from jax.sharding import PartitionSpec as P

FRAME_SAMPLES = 1024
FILTER_TAPS = 8
CHUNK_FRAMES = 4
RIM_CHUNKS = 2
SEND_ROWS = 16
TURN_ROWS = 256
TILE_ANTENNAS = 128
LANES = 128
VMEM_LIMIT = 58 * 2**20


def transform_table(length, window):
    turns = np.arange(length)[:, None] * np.arange(window)[None, :] % length
    angles = turns * (2.0 * np.pi / length)
    return np.concatenate([np.cos(angles), np.sin(angles)], axis=1).astype(np.float32)


def turn_matrix():
    matrix = np.zeros((TURN_ROWS, TURN_ROWS), np.float32)
    even = np.arange(0, TURN_ROWS, 2)
    matrix[even, even + 1] = 1.0
    matrix[even + 1, even] = -1.0
    return matrix


def spectra_kernel(
    sizes,
    taps_ref,
    table_ref,
    volts_ref,
    channel_ref,
    high,
    low,
    rows,
    total,
    spectra,
    turned,
    leaving,
    rim_out,
    rim_in,
    send_sem,
    recv_sem,
    own_sem,
    rim_send_sem,
    rim_recv_sem,
):
    groups, times, tiles, frames = sizes
    devices = groups * times * tiles
    step = pl.program_id(0)
    chunks = frames // CHUNK_FRAMES
    antennas = volts_ref.shape[0]
    width = table_ref.shape[1]
    window = width // 2
    frame_rows = 2 * antennas
    chunk_rows = CHUNK_FRAMES * frame_rows
    half = chunk_rows // 2
    group, time, tile = (lax.axis_index(axis) for axis in ("grp", "chan", "tile"))
    me = (group * times + time) * tiles + tile

    def place_of(device):
        return (
            lax.div(device, times * tiles),
            lax.rem(lax.div(device, tiles), times),
            lax.rem(device, tiles),
        )

    @pl.when(step == 0)
    def _():
        barrier = pltpu.get_barrier_semaphore()

        @pl.loop(1, devices)
        def _(distance):
            pl.semaphore_signal(
                barrier,
                inc=1,
                device_id=place_of(lax.rem(me + distance, devices)),
                device_id_type=pl.DeviceIdType.MESH,
            )

        total[...] = jnp.zeros_like(total)
        taps = taps_ref[...].T
        for tap in range(FILTER_TAPS):
            weights = taps[:, tap : tap + 1] * table_ref[...]
            upper = weights.astype(jnp.bfloat16)
            columns = pl.ds(tap * width, width)
            high[:, columns] = upper
            low[:, columns] = (weights - upper.astype(jnp.float32)).astype(jnp.bfloat16)

    chunk = chunks - 1 - step

    @pl.when(chunk >= 0)
    def _():
        for frame in range(CHUNK_FRAMES):
            rows[pl.ds(frame * frame_rows, frame_rows), :] = volts_ref[:, frame].reshape(
                frame_rows, FRAME_SAMPLES
            )
        for pair in range(FILTER_TAPS // 2):
            columns = pl.ds(2 * pair * width, 2 * width)
            product = jnp.dot(
                rows[...], high[:, columns], preferred_element_type=jnp.float32
            ) + jnp.dot(rows[...], low[:, columns], preferred_element_type=jnp.float32)
            for part in range(2):
                first = (chunk * CHUNK_FRAMES + 2 * pair + part) * frame_rows
                place = pl.ds(pl.multiple_of(first, frame_rows), chunk_rows)
                for lanes in range(width // LANES):
                    begin = part * width + lanes * LANES
                    total[lanes, place, :] += product[:, begin : begin + LANES]

    done = chunk + RIM_CHUNKS
    first = pl.multiple_of(done * chunk_rows, chunk_rows)

    def every_other(offset):
        place = pl.ds(first + offset, half, stride=2)
        return jnp.concatenate([total[i, place, :] for i in range(width // LANES)], axis=1)

    real, imaginary = every_other(0), every_other(1)
    lane = lax.broadcasted_iota(jnp.int32, (half, width), 1)
    signed = jnp.where(lane < window, real, -real)
    spectra[...] = signed + pltpu.roll(imaginary, window, 1)

    def rim_copy(slot):
        return pltpu.make_async_remote_copy(
            src_ref=rim_out.at[slot],
            dst_ref=rim_in.at[slot],
            send_sem=rim_send_sem.at[slot],
            recv_sem=rim_recv_sem.at[slot],
            device_id=(group, lax.rem(time + 1, times), tile),
            device_id_type=pl.DeviceIdType.MESH,
        )

    @pl.when(step == 0)
    def _():
        pl.semaphore_wait(pltpu.get_barrier_semaphore(), devices - 1)

    for slot in range(RIM_CHUNKS):

        @pl.when(done == chunks + slot)
        def _():
            rim_out[slot] = spectra[...]

            @pl.when(time < times - 1)
            def _():
                rim_copy(slot).start()

        @pl.when((done == slot) & (time > 0))
        def _():
            rim_copy(slot).wait_recv()
            spectra[...] += rim_in[slot]

    @pl.when(done < chunks)
    def _():
        late = lax.rem(done, 2)
        for frame in range(CHUNK_FRAMES):
            block = spectra[pl.ds(frame * antennas, antennas), :].T
            for part in range(2):
                row = (late * CHUNK_FRAMES + frame) * 2 + part
                turned[pl.ds(row, window, stride=SEND_ROWS), :] = block[
                    part * window : (part + 1) * window
                ]

    @pl.when((done < chunks) & (lax.rem(done, 2) == 0))
    def _():
        send = lax.div(done, 2)
        leaving[send] = turned[...].astype(jnp.bfloat16).reshape(leaving.shape[1:])
        top = pl.multiple_of(time * (2 * frames) + send * SEND_ROWS, SEND_ROWS)
        left = pl.multiple_of((group * tiles + tile) * antennas, antennas)
        landing = channel_ref.at[:, pl.ds(top, SEND_ROWS), pl.ds(left, antennas)]

        @pl.loop(1, devices)
        def _(distance):
            device = lax.rem(me + distance, devices)
            pltpu.make_async_remote_copy(
                src_ref=leaving.at[send, device],
                dst_ref=landing,
                send_sem=send_sem,
                recv_sem=recv_sem,
                device_id=place_of(device),
                device_id_type=pl.DeviceIdType.MESH,
            ).start()

        pltpu.make_async_copy(leaving.at[send, me], landing, own_sem.at[send]).start()

    @pl.when(done == 0)
    def _():
        for send in range(chunks // 2):
            top = pl.multiple_of(time * (2 * frames) + send * SEND_ROWS, SEND_ROWS)
            left = pl.multiple_of((group * tiles + tile) * antennas, antennas)
            landing = channel_ref.at[:, pl.ds(top, SEND_ROWS), pl.ds(left, antennas)]
            pltpu.make_async_copy(leaving.at[send, me], landing, own_sem.at[send]).wait()

        @pl.when(time < times - 1)
        def _():
            for slot in range(RIM_CHUNKS):
                rim_copy(slot).wait_send()

        others = leaving.at[:, pl.ds(0, devices - 1)]
        pltpu.make_async_copy(others, others, send_sem).wait()
        pltpu.make_async_copy(others, others, recv_sem).wait()


def spectra_by_channel(sizes, each, voltages, taps, table):
    groups, times, tiles = sizes
    devices = groups * times * tiles
    antennas, frames = voltages.shape[:2]
    width = table.shape[1]
    chunks = frames // CHUNK_FRAMES
    padded = frames + RIM_CHUNKS * CHUNK_FRAMES
    rim = (RIM_CHUNKS, CHUNK_FRAMES * antennas, width)
    weights = (FRAME_SAMPLES, FILTER_TAPS * width)
    return pl.pallas_call(
        functools.partial(spectra_kernel, (*sizes, frames)),
        grid=(chunks + RIM_CHUNKS,),
        out_shape=jax.ShapeDtypeStruct(
            (each, 2 * times * frames, groups * tiles * antennas), jnp.bfloat16
        ),
        in_specs=[
            pl.BlockSpec((FILTER_TAPS, FRAME_SAMPLES), lambda i: (0, 0)),
            pl.BlockSpec(
                (FRAME_SAMPLES, width), lambda i: (0, 0), pipeline_mode=pl.Buffered(1)
            ),
            pl.BlockSpec(
                (antennas, CHUNK_FRAMES, 2, FRAME_SAMPLES),
                lambda i: (0, jnp.maximum(chunks - 1 - i, 0), 0, 0),
            ),
        ],
        out_specs=pl.BlockSpec(memory_space=pl.ANY),
        scratch_shapes=[
            pltpu.VMEM(weights, jnp.bfloat16),
            pltpu.VMEM(weights, jnp.bfloat16),
            pltpu.VMEM((CHUNK_FRAMES * 2 * antennas, FRAME_SAMPLES), jnp.bfloat16),
            pltpu.VMEM((width // LANES, padded * 2 * antennas, LANES), jnp.float32),
            pltpu.VMEM(rim[1:], jnp.float32),
            pltpu.VMEM((width // 2 * SEND_ROWS, antennas), jnp.float32),
            pltpu.VMEM((chunks // 2, devices, each, SEND_ROWS, antennas), jnp.bfloat16),
            pltpu.VMEM(rim, jnp.float32),
            pltpu.VMEM(rim, jnp.float32),
            pltpu.SemaphoreType.DMA,
            pltpu.SemaphoreType.DMA,
            pltpu.SemaphoreType.DMA((chunks // 2,)),
            pltpu.SemaphoreType.DMA((RIM_CHUNKS,)),
            pltpu.SemaphoreType.DMA((RIM_CHUNKS,)),
        ],
        compiler_params=pltpu.CompilerParams(
            vmem_limit_bytes=VMEM_LIMIT, collective_id=0, has_side_effects=True
        ),
    )(taps, table, voltages)


def correlate_kernel(scale, blocks, turn_ref, channel_ref, real_ref, imaginary_ref):
    depth = channel_ref.shape[1]
    matrix = channel_ref[0]
    swapped = jnp.concatenate(
        [
            jnp.dot(
                turn_ref[...],
                matrix[top : top + TURN_ROWS],
                preferred_element_type=jnp.float32,
            ).astype(jnp.bfloat16)
            for top in range(0, depth, TURN_ROWS)
        ],
        axis=0,
    )
    pair = 0
    for i in range(blocks):
        here = slice(i * TILE_ANTENNAS, (i + 1) * TILE_ANTENNAS)
        left = jnp.concatenate([matrix[:, here], swapped[:, here]], axis=1)
        product = (
            lax.dot_general(
                left,
                matrix[:, i * TILE_ANTENNAS :],
                (((0,), (0,)), ((), ())),
                preferred_element_type=jnp.float32,
            )
            * scale
        )
        for j in range(blocks - i):
            there = slice(j * TILE_ANTENNAS, (j + 1) * TILE_ANTENNAS)
            real_ref[0, pair] = product[:TILE_ANTENNAS, there]
            imaginary_ref[0, pair] = product[TILE_ANTENNAS:, there]
            pair += 1


def correlate(channel_matrix, scale):
    channels, depth, antennas = channel_matrix.shape
    blocks = antennas // TILE_ANTENNAS
    pairs = blocks * (blocks + 1) // 2
    tiles = jax.ShapeDtypeStruct((channels, pairs, TILE_ANTENNAS, TILE_ANTENNAS), jnp.float32)
    tile_spec = pl.BlockSpec((1, pairs, TILE_ANTENNAS, TILE_ANTENNAS), lambda c: (c, 0, 0, 0))
    return pl.pallas_call(
        functools.partial(correlate_kernel, scale, blocks),
        grid=(channels,),
        out_shape=(tiles, tiles),
        in_specs=[
            pl.BlockSpec((TURN_ROWS, TURN_ROWS), lambda c: (0, 0)),
            pl.BlockSpec((1, depth, antennas), lambda c: (c, 0, 0)),
        ],
        out_specs=(tile_spec, tile_spec),
        compiler_params=pltpu.CompilerParams(vmem_limit_bytes=VMEM_LIMIT),
    )(jnp.asarray(turn_matrix(), jnp.bfloat16), channel_matrix)


def on_device(each, voltages, taps):
    sizes = tuple(lax.axis_size(axis) for axis in ("grp", "chan", "tile"))
    table = jnp.asarray(transform_table(FRAME_SAMPLES, each * math.prod(sizes)))
    channel_matrix = spectra_by_channel(sizes, each, voltages, taps, table)
    return correlate(channel_matrix, 1.0 / (sizes[1] * voltages.shape[1]))


def solution(mesh):
    split = ("grp", "chan", "tile")
    return jax.shard_map(
        functools.partial(on_device, 2),
        mesh=mesh,
        in_specs=(P(("grp", "tile"), "chan", None, None), P()),
        out_specs=(P(split, None, None, None), P(split, None, None, None)),
        check_vma=False,
    )
```

```python
import functools
import math

import jax
import jax.numpy as jnp
import numpy as np
from jax import lax
from jax.experimental import pallas as pl
from jax.experimental.pallas import tpu as pltpu
from jax.sharding import PartitionSpec as P

FRAME_SAMPLES = 1024
FILTER_TAPS = 8
CHUNK_FRAMES = 8
SEND_ROWS = 2 * CHUNK_FRAMES
BLOCK_TILES = 2
TURN_ROWS = 256
TILE_ANTENNAS = 128
LANES = 128
BLOCK_LANES = BLOCK_TILES * LANES
VMEM_LIMIT = 58 * 2**20


def transform_table(length, window):
    turns = np.arange(length)[:, None] * np.arange(window)[None, :] % length
    angles = turns * (2.0 * np.pi / length)
    return np.concatenate([np.cos(angles), np.sin(angles)], axis=1).astype(np.float32)


def turn_matrix():
    matrix = np.zeros((TURN_ROWS, TURN_ROWS), np.float32)
    even = np.arange(0, TURN_ROWS, 2)
    matrix[even, even + 1] = 1.0
    matrix[even + 1, even] = -1.0
    return matrix


def spectra_kernel(
    sizes,
    taps_ref,
    table_ref,
    volts_ref,
    channel_ref,
    high,
    low,
    rows,
    total,
    spectra,
    turned,
    leaving,
    rim_out,
    rim_in,
    send_sem,
    recv_sem,
    own_sem,
    rim_send_sem,
    rim_recv_sem,
):
    groups, times, tiles, frames = sizes
    devices = groups * times * tiles
    step = pl.program_id(0)
    chunks = frames // CHUNK_FRAMES
    antennas = volts_ref.shape[0]
    width = table_ref.shape[1]
    window = width // 2
    frame_rows = 2 * antennas
    chunk_rows = CHUNK_FRAMES * frame_rows
    half = chunk_rows // 2
    lane_tiles = width // LANES
    group, time, tile = (lax.axis_index(axis) for axis in ("grp", "chan", "tile"))
    me = (group * times + time) * tiles + tile

    def place_of(device):
        return (
            lax.div(device, times * tiles),
            lax.rem(lax.div(device, tiles), times),
            lax.rem(device, tiles),
        )

    @pl.when(step == 0)
    def _():
        barrier = pltpu.get_barrier_semaphore()

        @pl.loop(1, devices)
        def _(distance):
            pl.semaphore_signal(
                barrier,
                inc=1,
                device_id=place_of(lax.rem(me + distance, devices)),
                device_id_type=pl.DeviceIdType.MESH,
            )

        total[...] = jnp.zeros_like(total)
        taps = taps_ref[...].T
        for tap in range(FILTER_TAPS):
            weights = taps[:, tap : tap + 1] * table_ref[...]
            upper = weights.astype(jnp.bfloat16)
            columns = pl.ds(tap * width, width)
            high[:, columns] = upper
            low[:, columns] = (weights - upper.astype(jnp.float32)).astype(jnp.bfloat16)

    chunk = step - 1
    now, later = lax.rem(step + 1, 2), lax.rem(step, 2)

    def load_rows(skipped):
        for frame in range(skipped, CHUNK_FRAMES):
            rows[pl.ds(frame * frame_rows, frame_rows), :] = volts_ref[:, frame].reshape(
                frame_rows, FRAME_SAMPLES
            )

    def multiply(inside, outside, beyond):
        for block in range(FILTER_TAPS * width // BLOCK_LANES):
            tiles_here = range(block * BLOCK_TILES, (block + 1) * BLOCK_TILES)
            taps_here = [tile_here // lane_tiles for tile_here in tiles_here]
            begin = 0 if inside else chunk_rows - max(taps_here) * frame_rows
            end = chunk_rows if outside else chunk_rows - min(taps_here) * frame_rows
            if begin == end:
                continue
            columns = pl.ds(block * BLOCK_LANES, BLOCK_LANES)
            left = rows[begin:end, :]
            product = jnp.dot(
                left, high[:, columns], preferred_element_type=jnp.float32
            ) + jnp.dot(left, low[:, columns], preferred_element_type=jnp.float32)
            for part, tap in enumerate(taps_here):
                lanes = tiles_here[part] % lane_tiles
                own = slice(part * LANES, (part + 1) * LANES)
                shift = tap * frame_rows
                cut = chunk_rows - shift
                if inside:
                    total[now, lanes, shift:, :] += product[:cut, own]
                if outside and tap > 0:
                    total[beyond, lanes, :shift, :] += product[cut - begin :, own]

    @pl.when(step == 0)
    def _():
        load_rows(1)
        multiply(False, True, 1)

    @pl.when((step > 0) & (step < chunks))
    def _():
        total[later] = jnp.zeros(total.shape[1:], jnp.float32)
        load_rows(0)
        multiply(True, True, later)

    @pl.when(step == chunks)
    def _():
        load_rows(0)
        multiply(True, False, later)

    def finished(slot):
        def every_other(offset):
            place = pl.ds(offset, half, stride=2)
            return jnp.concatenate(
                [total[slot, i, place, :] for i in range(lane_tiles)], axis=1
            )

        real, imaginary = every_other(0), every_other(1)
        lane = lax.broadcasted_iota(jnp.int32, (half, width), 1)
        signed = jnp.where(lane < window, real, -real)
        return signed + pltpu.roll(imaginary, window, 1)

    rim_copy = pltpu.make_async_remote_copy(
        src_ref=rim_out,
        dst_ref=rim_in,
        send_sem=rim_send_sem,
        recv_sem=rim_recv_sem,
        device_id=(group, lax.rem(time + 1, times), tile),
        device_id_type=pl.DeviceIdType.MESH,
    )

    @pl.when(step == 0)
    def _():
        pl.semaphore_wait(pltpu.get_barrier_semaphore(), devices - 1)
        rim_out[...] = finished(1)[: rim_out.shape[0]]

        @pl.when(time < times - 1)
        def _():
            rim_copy.start()

    def landing(send):
        top = pl.multiple_of(time * (2 * frames) + send * SEND_ROWS, SEND_ROWS)
        left = pl.multiple_of((group * tiles + tile) * antennas, antennas)
        return channel_ref.at[:, pl.ds(top, SEND_ROWS), pl.ds(left, antennas)]

    @pl.when(step > 0)
    def _():
        spectra[...] = finished(now)

        @pl.when((step == 1) & (time > 0))
        def _():
            rim_copy.wait_recv()
            spectra[: rim_in.shape[0], :] += rim_in[...]

        for frame in range(CHUNK_FRAMES):
            block = spectra[pl.ds(frame * antennas, antennas), :].T
            for part in range(2):
                turned[pl.ds(frame * 2 + part, window, stride=SEND_ROWS), :] = block[
                    part * window : (part + 1) * window
                ]
        leaving[chunk] = turned[...].astype(jnp.bfloat16).reshape(leaving.shape[1:])

        @pl.loop(1, devices)
        def _(distance):
            device = lax.rem(me + distance, devices)
            pltpu.make_async_remote_copy(
                src_ref=leaving.at[chunk, device],
                dst_ref=landing(chunk),
                send_sem=send_sem,
                recv_sem=recv_sem,
                device_id=place_of(device),
                device_id_type=pl.DeviceIdType.MESH,
            ).start()

        pltpu.make_async_copy(leaving.at[chunk, me], landing(chunk), own_sem.at[chunk]).start()

    @pl.when(step == chunks)
    def _():
        for send in range(frames // CHUNK_FRAMES):
            pltpu.make_async_copy(leaving.at[send, me], landing(send), own_sem.at[send]).wait()

        @pl.when(time < times - 1)
        def _():
            rim_copy.wait_send()

        others = leaving.at[:, pl.ds(0, devices - 1)]
        pltpu.make_async_copy(others, others, send_sem).wait()
        pltpu.make_async_copy(others, others, recv_sem).wait()


def spectra_by_channel(sizes, each, voltages, taps, table):
    groups, times, tiles = sizes
    devices = groups * times * tiles
    antennas, frames = voltages.shape[:2]
    width = table.shape[1]
    chunks = frames // CHUNK_FRAMES
    rim = ((FILTER_TAPS - 1) * antennas, width)
    weights = (FRAME_SAMPLES, FILTER_TAPS * width)
    return pl.pallas_call(
        functools.partial(spectra_kernel, (*sizes, frames)),
        grid=(1 + chunks,),
        out_shape=jax.ShapeDtypeStruct(
            (each, 2 * times * frames, groups * tiles * antennas), jnp.bfloat16
        ),
        in_specs=[
            pl.BlockSpec((FILTER_TAPS, FRAME_SAMPLES), lambda i: (0, 0)),
            pl.BlockSpec(
                (FRAME_SAMPLES, width), lambda i: (0, 0), pipeline_mode=pl.Buffered(1)
            ),
            pl.BlockSpec(
                (antennas, CHUNK_FRAMES, 2, FRAME_SAMPLES),
                lambda i: (0, lax.rem(i + chunks - 1, chunks), 0, 0),
            ),
        ],
        out_specs=pl.BlockSpec(memory_space=pl.ANY),
        scratch_shapes=[
            pltpu.VMEM(weights, jnp.bfloat16),
            pltpu.VMEM(weights, jnp.bfloat16),
            pltpu.VMEM((CHUNK_FRAMES * 2 * antennas, FRAME_SAMPLES), jnp.bfloat16),
            pltpu.VMEM((2, width // LANES, CHUNK_FRAMES * 2 * antennas, LANES), jnp.float32),
            pltpu.VMEM((CHUNK_FRAMES * antennas, width), jnp.float32),
            pltpu.VMEM((width // 2 * SEND_ROWS, antennas), jnp.float32),
            pltpu.VMEM((chunks, devices, each, SEND_ROWS, antennas), jnp.bfloat16),
            pltpu.VMEM(rim, jnp.float32),
            pltpu.VMEM(rim, jnp.float32),
            pltpu.SemaphoreType.DMA,
            pltpu.SemaphoreType.DMA,
            pltpu.SemaphoreType.DMA((chunks,)),
            pltpu.SemaphoreType.DMA,
            pltpu.SemaphoreType.DMA,
        ],
        compiler_params=pltpu.CompilerParams(
            vmem_limit_bytes=VMEM_LIMIT, collective_id=0, has_side_effects=True
        ),
    )(taps, table, voltages)


def correlate_kernel(scale, blocks, turn_ref, channel_ref, real_ref, imaginary_ref):
    depth = channel_ref.shape[1]
    matrix = channel_ref[0]
    swapped = jnp.concatenate(
        [
            jnp.dot(
                turn_ref[...],
                matrix[top : top + TURN_ROWS],
                preferred_element_type=jnp.float32,
            ).astype(jnp.bfloat16)
            for top in range(0, depth, TURN_ROWS)
        ],
        axis=0,
    )
    pair = 0
    for i in range(blocks):
        here = slice(i * TILE_ANTENNAS, (i + 1) * TILE_ANTENNAS)
        left = jnp.concatenate([matrix[:, here], swapped[:, here]], axis=1)
        product = (
            lax.dot_general(
                left,
                matrix[:, i * TILE_ANTENNAS :],
                (((0,), (0,)), ((), ())),
                preferred_element_type=jnp.float32,
            )
            * scale
        )
        for j in range(blocks - i):
            there = slice(j * TILE_ANTENNAS, (j + 1) * TILE_ANTENNAS)
            real_ref[0, pair] = product[:TILE_ANTENNAS, there]
            imaginary_ref[0, pair] = product[TILE_ANTENNAS:, there]
            pair += 1


def correlate(channel_matrix, scale):
    channels, depth, antennas = channel_matrix.shape
    blocks = antennas // TILE_ANTENNAS
    pairs = blocks * (blocks + 1) // 2
    tiles = jax.ShapeDtypeStruct((channels, pairs, TILE_ANTENNAS, TILE_ANTENNAS), jnp.float32)
    tile_spec = pl.BlockSpec((1, pairs, TILE_ANTENNAS, TILE_ANTENNAS), lambda c: (c, 0, 0, 0))
    return pl.pallas_call(
        functools.partial(correlate_kernel, scale, blocks),
        grid=(channels,),
        out_shape=(tiles, tiles),
        in_specs=[
            pl.BlockSpec((TURN_ROWS, TURN_ROWS), lambda c: (0, 0)),
            pl.BlockSpec((1, depth, antennas), lambda c: (c, 0, 0)),
        ],
        out_specs=(tile_spec, tile_spec),
        compiler_params=pltpu.CompilerParams(vmem_limit_bytes=VMEM_LIMIT),
    )(jnp.asarray(turn_matrix(), jnp.bfloat16), channel_matrix)


def on_device(each, voltages, taps):
    sizes = tuple(lax.axis_size(axis) for axis in ("grp", "chan", "tile"))
    table = jnp.asarray(transform_table(FRAME_SAMPLES, each * math.prod(sizes)))
    channel_matrix = spectra_by_channel(sizes, each, voltages, taps, table)
    return correlate(channel_matrix, 1.0 / (sizes[1] * voltages.shape[1]))


def solution(mesh):
    split = ("grp", "chan", "tile")
    return jax.shard_map(
        functools.partial(on_device, 2),
        mesh=mesh,
        in_specs=(P(("grp", "tile"), "chan", None, None), P()),
        out_specs=(P(split, None, None, None), P(split, None, None, None)),
        check_vma=False,
    )
```

```python
import functools
import math

import jax
import jax.numpy as jnp
import numpy as np
from jax import lax
from jax.experimental import pallas as pl
from jax.experimental.pallas import tpu as pltpu
from jax.sharding import PartitionSpec as P

FRAME_SAMPLES = 1024
FILTER_TAPS = 8
CHUNK_FRAMES = 8
SEND_ROWS = 2 * CHUNK_FRAMES
BLOCK_TILES = 2
TURN_ROWS = 256
TILE_ANTENNAS = 128
LANES = 128
BLOCK_LANES = BLOCK_TILES * LANES
VMEM_LIMIT = 58 * 2**20


def transform_table(length, window):
    turns = np.arange(length)[:, None] * np.arange(window)[None, :] % length
    angles = turns * (2.0 * np.pi / length)
    return np.concatenate([np.cos(angles), np.sin(angles)], axis=1).astype(np.float32)


def turn_matrix():
    matrix = np.zeros((TURN_ROWS, TURN_ROWS), np.float32)
    even = np.arange(0, TURN_ROWS, 2)
    matrix[even, even + 1] = 1.0
    matrix[even + 1, even] = -1.0
    return matrix


def spectra_kernel(
    sizes,
    taps_ref,
    table_ref,
    volts_ref,
    channel_ref,
    high,
    low,
    rows,
    total,
    spectra,
    turned,
    leaving,
    rim_out,
    rim_in,
    send_sem,
    recv_sem,
    own_sem,
    rim_send_sem,
    rim_recv_sem,
):
    groups, times, tiles, frames = sizes
    devices = groups * times * tiles
    step = pl.program_id(0)
    chunks = frames // CHUNK_FRAMES
    antennas = volts_ref.shape[0]
    width = table_ref.shape[1]
    window = width // 2
    frame_rows = 2 * antennas
    chunk_rows = CHUNK_FRAMES * frame_rows
    half = chunk_rows // 2
    lane_tiles = width // LANES
    group, time, tile = (lax.axis_index(axis) for axis in ("grp", "chan", "tile"))
    me = (group * times + time) * tiles + tile

    def place_of(device):
        return (
            lax.div(device, times * tiles),
            lax.rem(lax.div(device, tiles), times),
            lax.rem(device, tiles),
        )

    @pl.when(step == 0)
    def _():
        barrier = pltpu.get_barrier_semaphore()

        @pl.loop(1, devices)
        def _(distance):
            pl.semaphore_signal(
                barrier,
                inc=1,
                device_id=place_of(lax.rem(me + distance, devices)),
                device_id_type=pl.DeviceIdType.MESH,
            )

        total[...] = jnp.zeros_like(total)
        taps = taps_ref[...].T
        for tap in range(FILTER_TAPS):
            weights = taps[:, tap : tap + 1] * table_ref[...]
            upper = weights.astype(jnp.bfloat16)
            columns = pl.ds(tap * width, width)
            high[:, columns] = upper
            low[:, columns] = (weights - upper.astype(jnp.float32)).astype(jnp.bfloat16)

    chunk = step - 1
    now, later = lax.rem(step + 1, 2), lax.rem(step, 2)

    def load_rows(skipped):
        for frame in range(skipped, CHUNK_FRAMES):
            rows[pl.ds(frame * frame_rows, frame_rows), :] = volts_ref[:, frame].reshape(
                frame_rows, FRAME_SAMPLES
            )

    def multiply(inside, outside, beyond):
        for block in range(FILTER_TAPS * width // BLOCK_LANES):
            tiles_here = range(block * BLOCK_TILES, (block + 1) * BLOCK_TILES)
            taps_here = [tile_here // lane_tiles for tile_here in tiles_here]
            begin = 0 if inside else chunk_rows - max(taps_here) * frame_rows
            end = chunk_rows if outside else chunk_rows - min(taps_here) * frame_rows
            if begin == end:
                continue
            columns = pl.ds(block * BLOCK_LANES, BLOCK_LANES)
            left = rows[begin:end, :]
            product = jnp.dot(
                left, high[:, columns], preferred_element_type=jnp.float32
            ) + jnp.dot(left, low[:, columns], preferred_element_type=jnp.float32)
            for part, tap in enumerate(taps_here):
                lanes = tiles_here[part] % lane_tiles
                own = slice(part * LANES, (part + 1) * LANES)
                shift = tap * frame_rows
                cut = chunk_rows - shift
                if inside:
                    total[now, lanes, shift:, :] += product[:cut, own]
                if outside and tap > 0:
                    total[beyond, lanes, :shift, :] += product[cut - begin :, own]

    @pl.when(step == 0)
    def _():
        load_rows(1)
        multiply(False, True, 1)

    @pl.when((step > 0) & (step < chunks))
    def _():
        total[later] = jnp.zeros(total.shape[1:], jnp.float32)
        load_rows(0)
        multiply(True, True, later)

    @pl.when(step == chunks)
    def _():
        load_rows(0)
        multiply(True, False, later)

    def finished(slot):
        def every_other(offset):
            place = pl.ds(offset, half, stride=2)
            return jnp.concatenate(
                [total[slot, i, place, :] for i in range(lane_tiles)], axis=1
            )

        real, imaginary = every_other(0), every_other(1)
        lane = lax.broadcasted_iota(jnp.int32, (half, width), 1)
        signed = jnp.where(lane < window, real, -real)
        return signed + pltpu.roll(imaginary, window, 1)

    rim_copy = pltpu.make_async_remote_copy(
        src_ref=rim_out,
        dst_ref=rim_in,
        send_sem=rim_send_sem,
        recv_sem=rim_recv_sem,
        device_id=(group, lax.rem(time + 1, times), tile),
        device_id_type=pl.DeviceIdType.MESH,
    )

    @pl.when(step == 0)
    def _():
        pl.semaphore_wait(pltpu.get_barrier_semaphore(), devices - 1)
        rim_out[...] = finished(1)[: rim_out.shape[0]]

        @pl.when(time < times - 1)
        def _():
            rim_copy.start()

    def landing(send):
        top = pl.multiple_of(time * (2 * frames) + send * SEND_ROWS, SEND_ROWS)
        left = pl.multiple_of((group * tiles + tile) * antennas, antennas)
        return channel_ref.at[:, pl.ds(top, SEND_ROWS), pl.ds(left, antennas)]

    @pl.when(step > 0)
    def _():
        spectra[...] = finished(now)

        @pl.when((step == 1) & (time > 0))
        def _():
            rim_copy.wait_recv()
            spectra[: rim_in.shape[0], :] += rim_in[...]

        for frame in range(CHUNK_FRAMES):
            block = spectra[pl.ds(frame * antennas, antennas), :].T
            for part in range(2):
                turned[pl.ds(frame * 2 + part, window, stride=SEND_ROWS), :] = block[
                    part * window : (part + 1) * window
                ]
        leaving[chunk] = turned[...].astype(jnp.bfloat16).reshape(leaving.shape[1:])

        @pl.loop(1, devices, unroll=True)
        def _(distance):
            device = lax.rem(me + distance, devices)
            pltpu.make_async_remote_copy(
                src_ref=leaving.at[chunk, device],
                dst_ref=landing(chunk),
                send_sem=send_sem,
                recv_sem=recv_sem,
                device_id=place_of(device),
                device_id_type=pl.DeviceIdType.MESH,
            ).start()

        pltpu.make_async_copy(leaving.at[chunk, me], landing(chunk), own_sem.at[chunk]).start()

    @pl.when(step == chunks)
    def _():
        for send in range(frames // CHUNK_FRAMES):
            pltpu.make_async_copy(leaving.at[send, me], landing(send), own_sem.at[send]).wait()

        @pl.when(time < times - 1)
        def _():
            rim_copy.wait_send()

        others = leaving.at[:, pl.ds(0, devices - 1)]
        pltpu.make_async_copy(others, others, send_sem).wait()
        pltpu.make_async_copy(others, others, recv_sem).wait()


def spectra_by_channel(sizes, each, voltages, taps, table):
    groups, times, tiles = sizes
    devices = groups * times * tiles
    antennas, frames = voltages.shape[:2]
    width = table.shape[1]
    chunks = frames // CHUNK_FRAMES
    rim = ((FILTER_TAPS - 1) * antennas, width)
    weights = (FRAME_SAMPLES, FILTER_TAPS * width)
    return pl.pallas_call(
        functools.partial(spectra_kernel, (*sizes, frames)),
        grid=(1 + chunks,),
        out_shape=jax.ShapeDtypeStruct(
            (each, 2 * times * frames, groups * tiles * antennas), jnp.bfloat16
        ),
        in_specs=[
            pl.BlockSpec((FILTER_TAPS, FRAME_SAMPLES), lambda i: (0, 0)),
            pl.BlockSpec(
                (FRAME_SAMPLES, width), lambda i: (0, 0), pipeline_mode=pl.Buffered(1)
            ),
            pl.BlockSpec(
                (antennas, CHUNK_FRAMES, 2, FRAME_SAMPLES),
                lambda i: (0, lax.rem(i + chunks - 1, chunks), 0, 0),
            ),
        ],
        out_specs=pl.BlockSpec(memory_space=pl.ANY),
        scratch_shapes=[
            pltpu.VMEM(weights, jnp.bfloat16),
            pltpu.VMEM(weights, jnp.bfloat16),
            pltpu.VMEM((CHUNK_FRAMES * 2 * antennas, FRAME_SAMPLES), jnp.bfloat16),
            pltpu.VMEM((2, width // LANES, CHUNK_FRAMES * 2 * antennas, LANES), jnp.float32),
            pltpu.VMEM((CHUNK_FRAMES * antennas, width), jnp.float32),
            pltpu.VMEM((width // 2 * SEND_ROWS, antennas), jnp.float32),
            pltpu.VMEM((chunks, devices, each, SEND_ROWS, antennas), jnp.bfloat16),
            pltpu.VMEM(rim, jnp.float32),
            pltpu.VMEM(rim, jnp.float32),
            pltpu.SemaphoreType.DMA,
            pltpu.SemaphoreType.DMA,
            pltpu.SemaphoreType.DMA((chunks,)),
            pltpu.SemaphoreType.DMA,
            pltpu.SemaphoreType.DMA,
        ],
        compiler_params=pltpu.CompilerParams(
            vmem_limit_bytes=VMEM_LIMIT, collective_id=0, has_side_effects=True
        ),
    )(taps, table, voltages)


def correlate_kernel(scale, blocks, turn_ref, channel_ref, real_ref, imaginary_ref):
    depth = channel_ref.shape[1]
    matrix = channel_ref[0]
    swapped = jnp.concatenate(
        [
            jnp.dot(
                turn_ref[...],
                matrix[top : top + TURN_ROWS],
                preferred_element_type=jnp.float32,
            ).astype(jnp.bfloat16)
            for top in range(0, depth, TURN_ROWS)
        ],
        axis=0,
    )
    pair = 0
    for i in range(blocks):
        here = slice(i * TILE_ANTENNAS, (i + 1) * TILE_ANTENNAS)
        left = jnp.concatenate([matrix[:, here], swapped[:, here]], axis=1)
        product = (
            lax.dot_general(
                left,
                matrix[:, i * TILE_ANTENNAS :],
                (((0,), (0,)), ((), ())),
                preferred_element_type=jnp.float32,
            )
            * scale
        )
        for j in range(blocks - i):
            there = slice(j * TILE_ANTENNAS, (j + 1) * TILE_ANTENNAS)
            real_ref[0, pair] = product[:TILE_ANTENNAS, there]
            imaginary_ref[0, pair] = product[TILE_ANTENNAS:, there]
            pair += 1


def correlate(channel_matrix, scale):
    channels, depth, antennas = channel_matrix.shape
    blocks = antennas // TILE_ANTENNAS
    pairs = blocks * (blocks + 1) // 2
    tiles = jax.ShapeDtypeStruct((channels, pairs, TILE_ANTENNAS, TILE_ANTENNAS), jnp.float32)
    tile_spec = pl.BlockSpec((1, pairs, TILE_ANTENNAS, TILE_ANTENNAS), lambda c: (c, 0, 0, 0))
    return pl.pallas_call(
        functools.partial(correlate_kernel, scale, blocks),
        grid=(channels,),
        out_shape=(tiles, tiles),
        in_specs=[
            pl.BlockSpec((TURN_ROWS, TURN_ROWS), lambda c: (0, 0)),
            pl.BlockSpec((1, depth, antennas), lambda c: (c, 0, 0)),
        ],
        out_specs=(tile_spec, tile_spec),
        compiler_params=pltpu.CompilerParams(vmem_limit_bytes=VMEM_LIMIT),
    )(jnp.asarray(turn_matrix(), jnp.bfloat16), channel_matrix)


def on_device(each, voltages, taps):
    sizes = tuple(lax.axis_size(axis) for axis in ("grp", "chan", "tile"))
    table = jnp.asarray(transform_table(FRAME_SAMPLES, each * math.prod(sizes)))
    channel_matrix = spectra_by_channel(sizes, each, voltages, taps, table)
    return correlate(channel_matrix, 1.0 / (sizes[1] * voltages.shape[1]))


def solution(mesh):
    split = ("grp", "chan", "tile")
    return jax.shard_map(
        functools.partial(on_device, 2),
        mesh=mesh,
        in_specs=(P(("grp", "tile"), "chan", None, None), P()),
        out_specs=(P(split, None, None, None), P(split, None, None, None)),
        check_vma=False,
    )
```
